256 devices in a mesh: patch: 4 (over x_hi, core), seq: 64 (over y, z, x_lo).
Axes of the slice: x: 4 (x_hi: 2, x_lo: 2; x = x_hi * 2 + x_lo), y: 4, z: 8, core: 2. Of those that a mesh axis runs over, the one named last changes fastest.
Arguments:
- fresh_qkv: bfloat16 [3, 4608, 192, 128], P(None, ('patch', 'seq')), as said below
- stale_kv: bfloat16 [2, 4608, 192, 128], P(None, None, 'seq'), may hold values from -6 to 6
- text_count: int32 [8], replicated, may hold values from 128 to 512
Outputs:
- attended: bfloat16 [4608, 192, 128], P(('patch', 'seq'))
- refreshed_kv: bfloat16 [2, 4608, 192, 128], P(None, None, 'seq')
The draws below stay inside these ranges and needn't reach their ends.
Inputs may be any that keep to these rules, and one draw needn't show every extreme that they name: `fresh_qkv`: each entry lies within -100 to 100.
All inputs are finite; a program needn't handle non-finite values.
Results may differ from the reference program's by a relative error of at most 0.0049.
Values may be sent and summed in bfloat16 or wider, within the bound.
No kernel may reach another device: no remote copies, remote signals or barrier semaphores. Data moves between devices by JAX's collectives and lax.ppermute only.
A program may use at most 128 MiB of HBM per device.

```python
import math
import jax
import jax.numpy as jnp
from jax import lax

HEADS = 24
HDIM = 128
IMAGES = 8
TXT = 512
SEQ = 4608
N_PATCH = 4


def draw_fresh_qkv(key, part):
    key = jax.random.fold_in(key, 11)
    key_base = jax.random.fold_in(key, 0)
    shape = (3, SEQ, IMAGES * HEADS, HDIM)
    base = jax.random.normal(key_base, shape, jnp.float32)
    return base.astype(jnp.bfloat16)


def set_ends(array, rng, least, high):
    shape = array.shape
    index_at = [jax.random.randint(jax.random.fold_in(rng, axis), (), 0, shape[axis]) for axis in range(len(shape))]
    array = array.at[tuple(index_at)].set(least)
    longest = shape.index(max(shape))
    index_at[longest] = (index_at[longest] + 1) % shape[longest]
    return array.at[tuple(index_at)].set(high)


def block_scale(rng, shape, cuts, low, high):
    level = 1.0
    for dim, parts in cuts:
        steps = jax.random.uniform(jax.random.fold_in(jax.random.fold_in(rng, 6), dim), (parts,), jnp.float32, low / len(cuts), high / len(cuts))
        level = level * jnp.repeat(jnp.exp(steps), shape[dim] // parts).reshape((-1,) + (1,) * (len(shape) - 1 - dim))
    return level


def normal_values(key, shape, width, limit, shards=(), dtype=jnp.bfloat16):
    entries = width * jax.random.normal(key, shape, jnp.float32)
    if shards:
        entries = entries * block_scale(key, shape, shards, -0.22, 0.18)
    return jnp.clip(entries, -limit, limit).astype(dtype)


def setup_inputs(seed: int = 0) -> dict:
    seeds = jax.random.split(jax.random.key(seed), 4)
    fresh_qkv = draw_fresh_qkv(jax.random.fold_in(seeds[3], 71), 0)
    stale_kv = normal_values(seeds[1], (2, SEQ, IMAGES * HEADS, HDIM), 1.0, 6.0, ((2, 64),))
    text_count = set_ends(jax.random.randint(seeds[2], (IMAGES,), TXT // 4, TXT + 1), jax.random.fold_in(seeds[2], 1), TXT // 4, TXT).astype(jnp.int32)
    return dict(fresh_qkv=fresh_qkv, stale_kv=stale_kv, text_count=text_count)


def reference(fresh_qkv, stale_kv, text_count):
    pair_count = fresh_qkv.shape[2]
    patch_len = SEQ // N_PATCH
    score_scale = 1.0 / math.sqrt(HDIM)
    fresh_pairs = jnp.transpose(fresh_qkv, (2, 0, 1, 3))
    stale_pairs = jnp.transpose(stale_kv, (2, 0, 1, 3))
    image_index = jnp.arange(pair_count) // HEADS
    valid_counts = text_count[image_index]
    position = jnp.arange(SEQ)

    def per_pair(operands):
        fresh_block, stale_block, valid_text = operands
        visible = (position >= TXT) | (position < valid_text)
        pieces = []
        for group in range(N_PATCH):
            start = group * patch_len
            key_block = stale_block[0].at[start:start + patch_len].set(fresh_block[1, start:start + patch_len])
            value_block = stale_block[1].at[start:start + patch_len].set(fresh_block[2, start:start + patch_len])
            query_rows = fresh_block[0, start:start + patch_len]
            scores = jnp.dot(query_rows, key_block.T, preferred_element_type=jnp.float32) * score_scale
            scores = jnp.where(visible[None, :], scores, -jnp.inf)
            highest = lax.optimization_barrier(jnp.max(scores, axis=1, keepdims=True))
            raised = jnp.exp(scores - highest)
            weights = (raised / lax.optimization_barrier(jnp.sum(raised, axis=1, keepdims=True))).astype(jnp.bfloat16)
            pieces.append(jnp.dot(weights, value_block, preferred_element_type=jnp.float32).astype(jnp.bfloat16))
        return jnp.concatenate(pieces, axis=0)
    outputs = jax.lax.map(per_pair, (fresh_pairs, stale_pairs, valid_counts))
    attended = jnp.transpose(outputs, (1, 0, 2))
    return (attended, fresh_qkv[1:3])
```

```python
import functools
import math

import jax
import jax.numpy as jnp
from jax import lax
from jax.experimental import pallas as pl
from jax.experimental.pallas import tpu as pltpu
from jax.sharding import PartitionSpec as P

HEADS = 24
TXT_DEV = 2
IMG_DEV = 16
KINDS = 3
BLOCK = 384
MIB = 1024 * 1024
F32 = jnp.float32
VMEM = pl.BlockSpec(memory_space=pltpu.VMEM)


def cost(mib, flops=0, exps=0):
    return pl.CostEstimate(flops=flops, bytes_accessed=mib * MIB, transcendentals=exps)


def pack_kernel(here, x_ref, o_ref, read, wide, sent, packed, in_sems, out_sems):
    kinds, tokens, pairs, _ = x_ref.shape
    steps = in_sems.shape[0]
    columns = pairs // steps
    peers = columns // here
    rows = kinds * tokens * here
    reads, writes = [], []
    for i in range(steps):
        part = pl.ds(i * columns, columns)
        copy = pltpu.make_async_copy(x_ref.at[:, :, part, :], read.at[i], in_sems.at[i])
        copy.start()
        reads.append(copy)
    for i in range(steps):
        reads[i].wait()
        wide[...] = read[i].astype(F32).reshape(wide.shape)
        for c in range(kinds):
            for t in range(tokens):
                for j in range(here):
                    first = (c * tokens + t) * columns + j
                    row = (j * kinds + c) * tokens + t
                    sent[pl.ds(row, peers, stride=rows), :] = wide[pl.ds(first, peers, stride=here), :]
        packed[i] = sent[...].astype(packed.dtype)
        part = pl.ds(i * peers * rows, peers * rows)
        copy = pltpu.make_async_copy(packed.at[i], o_ref.at[part, :], out_sems.at[i])
        copy.start()
        writes.append(copy)
    for copy in writes:
        copy.wait()


PACK_STEPS = 4


def pack(fresh_qkv, peers):
    kinds, tokens, pairs, width = fresh_qkv.shape
    columns = pairs // PACK_STEPS
    part = (kinds * tokens * columns, width)
    anywhere = pl.BlockSpec(memory_space=pl.ANY)
    return pl.pallas_call(
        functools.partial(pack_kernel, pairs // peers),
        out_shape=jax.ShapeDtypeStruct((kinds * tokens * pairs, width), fresh_qkv.dtype),
        in_specs=[anywhere],
        out_specs=anywhere,
        scratch_shapes=[
            pltpu.VMEM((PACK_STEPS, kinds, tokens, columns, width), fresh_qkv.dtype),
            pltpu.VMEM(part, F32),
            pltpu.VMEM(part, F32),
            pltpu.VMEM((PACK_STEPS, *part), fresh_qkv.dtype),
            pltpu.SemaphoreType.DMA((PACK_STEPS,)),
            pltpu.SemaphoreType.DMA((PACK_STEPS,)),
        ],
        compiler_params=pltpu.CompilerParams(vmem_limit_bytes=60 * MIB),
        cost_estimate=cost(6),
        name="pack",
    )(fresh_qkv)


def unpack_kernel(kinds, x_ref, o_ref, wide, ordered):
    count, here, length, _ = o_ref.shape
    rows = KINDS * here
    total = x_ref.shape[0]
    wide[...] = x_ref[...].astype(F32)
    tokens = TOKENS
    peers = length // tokens
    for c, kind in enumerate(kinds):
        for j in range(here):
            for t in range(tokens):
                row = (j * KINDS + kind) * tokens + t
                block = wide[pl.ds(row, peers, stride=rows * tokens), :]
                ordered[c * here + j, pl.ds(t, peers, stride=tokens), :] = block
    o_ref[...] = ordered[...].reshape(o_ref.shape).astype(o_ref.dtype)


TOKENS = 18


def unpack(received, here, kinds):
    total, width = received.shape
    length = total // (KINDS * here)
    return pl.pallas_call(
        functools.partial(unpack_kernel, kinds),
        out_shape=jax.ShapeDtypeStruct((len(kinds), here, length, width), received.dtype),
        in_specs=[VMEM],
        out_specs=VMEM,
        scratch_shapes=[
            pltpu.VMEM((total, width), F32),
            pltpu.VMEM((len(kinds) * here, length, width), F32),
        ],
        compiler_params=pltpu.CompilerParams(vmem_limit_bytes=24 * MIB),
        cost_estimate=cost(5),
        name="unpack",
    )(received)


def hide_text(valid, text, keys, values, width, first):
    length = text.size
    shown = lax.broadcasted_iota(jnp.int32, (length, width), 0) < valid
    keys[text, :] = jnp.where(shown, keys[text, :].astype(F32), first).astype(keys.dtype)
    for part in range(2):
        lanes = pl.ds(part * width, width)
        values[text, lanes] = jnp.where(shown, values[text, lanes].astype(F32), 0.0).astype(values.dtype)


def prepare_kernel(text_len, scalars, stale_ref, keys, values, sems):
    pair = pl.program_id(0)
    width = keys.shape[-1]
    groups = sems.shape[1] + 1
    length = keys.shape[1] // (groups - 1)
    own = scalars[0]
    valid = scalars[1 + pair]
    copies = []
    for step in range(1, groups):
        group = lax.rem(own + step, groups)
        source = pl.ds(pl.multiple_of(group * length, length), length)
        rows = pl.ds((step - 1) * length, length)
        for which, target in ((0, keys.at[0, rows, :]), (1, values.at[0, rows, pl.ds(0, width)])):
            copy = pltpu.make_async_copy(
                stale_ref.at[which, pair, source, :], target, sems.at[which, step - 1]
            )
            copy.start()
            copies.append(copy)
    values[0, :, pl.ds(width, width)] = jnp.ones((keys.shape[1], width), values.dtype)
    for copy in copies:
        copy.wait()

    @pl.when(own > 0)
    def _():
        start = pl.multiple_of((groups - 1 - own) * length, length)
        first = keys[0, pl.ds(start, 16), :][0:1].astype(F32)
        hide_text(valid, pl.ds(start, text_len), keys.at[0], values.at[0], width, first)


def prepare(scalars, stale, groups, text_len):
    _, here, seq_len, width = stale.shape
    others = seq_len // groups * (groups - 1)
    return pl.pallas_call(
        functools.partial(prepare_kernel, text_len),
        grid=(here,),
        out_shape=[
            jax.ShapeDtypeStruct((here, others, width), stale.dtype),
            jax.ShapeDtypeStruct((here, others, 2 * width), stale.dtype),
        ],
        in_specs=[
            pl.BlockSpec(memory_space=pltpu.SMEM),
            pl.BlockSpec(memory_space=pl.ANY),
        ],
        out_specs=[
            pl.BlockSpec((1, others, width), lambda i: (i, 0, 0)),
            pl.BlockSpec((1, others, 2 * width), lambda i: (i, 0, 0)),
        ],
        scratch_shapes=[pltpu.SemaphoreType.DMA((2, groups - 1))],
        compiler_params=pltpu.CompilerParams(vmem_limit_bytes=16 * MIB),
        cost_estimate=cost(64),
        name="prepare",
    )(scalars, stale)


def attend_kernel(text_len, tokens, scalars, q_ref, fresh_ref, old_keys, old_values, o_ref,
                  keys, values, scores, highest, result, sent):
    here, length, width = q_ref.shape
    peers = length // tokens
    blocks = length // BLOCK
    scale = math.log2(math.e) / math.sqrt(width)
    own = scalars[0]
    values[:, pl.ds(width, width)] = jnp.ones((length, width), values.dtype)

    def attend_pair(pair, _):
        valid = scalars[1 + pair]
        keys[...] = fresh_ref[0, pair]
        values[:, pl.ds(0, width)] = fresh_ref[1, pair]

        @pl.when(own == 0)
        def _():
            values[pl.ds(0, text_len), pl.ds(width, width)] = jnp.ones((text_len, width), values.dtype)
            first = keys[0:16, :][0:1].astype(F32)
            hide_text(valid, pl.ds(0, text_len), keys, values, width, first)

        def score(i, slot):
            query = q_ref[pair, pl.ds(i * BLOCK, BLOCK), :]
            dims = (((1,), (1,)), ((), ()))
            new = lax.dot_general(query, keys[...], dims, preferred_element_type=F32)
            old = lax.dot_general(query, old_keys[pair], dims, preferred_element_type=F32)
            scores[slot, :, pl.ds(0, length)] = new
            scores[slot, :, pl.ds(length, old.shape[1])] = old
            top = jnp.maximum(
                jnp.max(new, axis=1, keepdims=True), jnp.max(old, axis=1, keepdims=True)
            )
            highest[slot] = jnp.broadcast_to(top, (BLOCK, width))

        def weigh(i, slot):
            top = highest[slot][:, :1]
            weights = jnp.exp2((scores[slot] - top) * scale).astype(values.dtype)
            summed = jnp.dot(weights[:, :length], values[...], preferred_element_type=F32)
            summed += jnp.dot(weights[:, length:], old_values[pair], preferred_element_type=F32)
            result[pl.ds(i * BLOCK, BLOCK), :] = summed[:, :width] / summed[:, width:]

        score(0, 0)
        for i in range(1, blocks):
            score(i, i % 2)
            weigh(i - 1, (i - 1) % 2)
        weigh(blocks - 1, (blocks - 1) % 2)
        for t in range(tokens):
            rows = pl.ds(pair * tokens + t, peers, stride=here * tokens)
            sent[rows, :] = result[pl.ds(t, peers, stride=tokens), :]
        return 0

    lax.fori_loop(0, here, attend_pair, 0)
    o_ref[...] = sent[...].astype(o_ref.dtype)


PAIRS = 3


def attend(scalars, query, fresh, old_keys, old_values, text_len, tokens):
    here, length, width = query.shape
    others = old_keys.shape[1]
    total = length + others
    return pl.pallas_call(
        functools.partial(attend_kernel, text_len, tokens),
        out_shape=jax.ShapeDtypeStruct((here * length, width), query.dtype),
        in_specs=[pl.BlockSpec(memory_space=pltpu.SMEM)] + [VMEM] * 4,
        out_specs=VMEM,
        scratch_shapes=[
            pltpu.VMEM((length, width), query.dtype),
            pltpu.VMEM((length, 2 * width), query.dtype),
            pltpu.VMEM((2, BLOCK, total), F32),
            pltpu.VMEM((2, BLOCK, width), F32),
            pltpu.VMEM((length, width), F32),
            pltpu.VMEM((here * length, width), F32),
        ],
        compiler_params=pltpu.CompilerParams(vmem_limit_bytes=40 * MIB),
        cost_estimate=cost(16, 8 * here * length * total * width, here * length * total),
        name="attend",
    )(scalars, query, fresh, old_keys, old_values)


def merge_kernel(x_ref, o_ref, wide, spread):
    tokens, pairs, _ = o_ref.shape
    here = PAIRS
    peers = pairs // here
    wide[...] = x_ref[...].astype(F32)
    for j in range(here):
        for t in range(tokens):
            block = wide[pl.ds(j * tokens + t, peers, stride=here * tokens), :]
            spread[pl.ds(t * pairs + j, peers, stride=here), :] = block
    o_ref[...] = spread[...].reshape(o_ref.shape).astype(o_ref.dtype)


def merge(moved, pairs):
    total, width = moved.shape
    return pl.pallas_call(
        merge_kernel,
        out_shape=jax.ShapeDtypeStruct((total // pairs, pairs, width), moved.dtype),
        in_specs=[VMEM],
        out_specs=VMEM,
        scratch_shapes=[pltpu.VMEM((total, width), F32)] * 2,
        compiler_params=pltpu.CompilerParams(vmem_limit_bytes=16 * MIB),
        cost_estimate=cost(2),
        name="merge",
    )(moved)


def place_kernel(scalars, *refs):
    part_refs, o_ref = refs[:-1], refs[-1]
    length = part_refs[0].shape[2]
    for step, part_ref in enumerate(part_refs):
        group = jnp.bitwise_xor(scalars[0], step)
        o_ref[0, 0, pl.ds(pl.multiple_of(group * length, length), length), :] = part_ref[0, 0]


def place(scalars, parts):
    kinds, here, length, width = parts[0].shape
    total = len(parts) * length
    block = lambda i, j: (i, j, 0, 0)
    return pl.pallas_call(
        place_kernel,
        grid=(kinds, here),
        out_shape=jax.ShapeDtypeStruct((kinds, here, total, width), parts[0].dtype),
        in_specs=[pl.BlockSpec(memory_space=pltpu.SMEM)]
        + [pl.BlockSpec((1, 1, length, width), block)] * len(parts),
        out_specs=pl.BlockSpec((1, 1, total, width), block),
        compiler_params=pltpu.CompilerParams(vmem_limit_bytes=16 * MIB),
        cost_estimate=cost(0),
        name="place",
    )(scalars, *parts)


def exchange(rows):
    two_rows = rows.reshape(rows.shape[0] // 2, 2, rows.shape[1])
    moved = lax.all_to_all(two_rows, "seq", split_axis=0, concat_axis=0, tiled=True)
    return moved.reshape(rows.shape)


def swap(array, bit):
    groups = lax.axis_size("patch")
    return lax.ppermute(array, "patch", [(g, g ^ bit) for g in range(groups)])


def per_device(fresh_qkv, stale_kv, text_count):
    peers = lax.axis_size("seq")
    groups = lax.axis_size("patch")
    tokens, pairs = fresh_qkv.shape[1:3]
    here = pairs // peers
    seq_len = stale_kv.shape[1]
    text_len = TXT_DEV * seq_len // (TXT_DEV + IMG_DEV)
    first_pair = lax.axis_index("seq") * here
    image_index = (first_pair + jnp.arange(here)) // HEADS
    matches = image_index[:, None] == jnp.arange(text_count.shape[0])[None, :]
    valid_counts = jnp.sum(jnp.where(matches, text_count[None, :], 0), axis=1)
    own = lax.axis_index("patch").astype(jnp.int32)
    scalars = jnp.concatenate([own[None], valid_counts.astype(jnp.int32)])
    stale = jnp.transpose(stale_kv, (0, 2, 1, 3))

    sent, scalars = lax.optimization_barrier((pack(fresh_qkv, peers), scalars))
    received = exchange(sent)
    old_keys, old_values = prepare(scalars, stale, groups, text_len)
    received, old_keys, old_values = lax.optimization_barrier((received, old_keys, old_values))

    fresh = unpack(received, here, (1, 2))
    far = swap(fresh, 2)
    query = unpack(received, here, (0,))[0]
    attended = attend(scalars, query, fresh, old_keys, old_values, text_len, tokens)
    moved = exchange(attended)
    far, _ = lax.optimization_barrier((far, attended))
    near, far_near = swap(fresh, 1), swap(far, 1)
    refreshed = place(scalars, [fresh, near, far, far_near])
    moved, refreshed = lax.optimization_barrier((moved, refreshed))
    result = merge(moved, pairs)
    return (result, jnp.transpose(refreshed, (0, 2, 1, 3)))


def solution(mesh):
    in_specs = (P(None, ("patch", "seq"), None, None), P(None, None, "seq", None), P())
    out_specs = (P(("patch", "seq"), None, None), P(None, None, "seq", None))
    return jax.shard_map(
        per_device, mesh=mesh, in_specs=in_specs, out_specs=out_specs, check_vma=False
    )
```

```python
import functools
import math

import jax
import jax.numpy as jnp
from jax import lax
from jax.experimental import pallas as pl
from jax.experimental.pallas import tpu as pltpu
from jax.sharding import PartitionSpec as P

HEADS = 24
TXT_DEV = 2
IMG_DEV = 16
KINDS = 3
BLOCK = 384
MIB = 1024 * 1024
F32 = jnp.float32
VMEM = pl.BlockSpec(memory_space=pltpu.VMEM)
ANY = pl.BlockSpec(memory_space=pl.ANY)


def cost(mib, flops=0, exps=0):
    return pl.CostEstimate(flops=flops, bytes_accessed=mib * MIB, transcendentals=exps)


def pack_kernel(here, x_ref, o_ref, read, wide, sent, packed, in_sems, out_sems):
    kinds, tokens, pairs, _ = x_ref.shape
    steps = in_sems.shape[0]
    columns = pairs // steps
    peers = columns // here
    rows = kinds * tokens * here
    reads, writes = [], []
    for i in range(steps):
        part = pl.ds(i * columns, columns)
        copy = pltpu.make_async_copy(x_ref.at[:, :, part, :], read.at[i], in_sems.at[i])
        copy.start()
        reads.append(copy)
    for i in range(steps):
        reads[i].wait()
        wide[...] = read[i].astype(F32).reshape(wide.shape)
        for c in range(kinds):
            for t in range(tokens):
                for j in range(here):
                    first = (c * tokens + t) * columns + j
                    row = (j * kinds + c) * tokens + t
                    sent[pl.ds(row, peers, stride=rows), :] = wide[pl.ds(first, peers, stride=here), :]
        packed[i] = sent[...].astype(packed.dtype)
        part = pl.ds(i * peers * rows, peers * rows)
        copy = pltpu.make_async_copy(packed.at[i], o_ref.at[part, :], out_sems.at[i])
        copy.start()
        writes.append(copy)
    for copy in writes:
        copy.wait()


PACK_STEPS = 4


def pack(fresh_qkv, peers):
    kinds, tokens, pairs, width = fresh_qkv.shape
    columns = pairs // PACK_STEPS
    part = (kinds * tokens * columns, width)
    return pl.pallas_call(
        functools.partial(pack_kernel, pairs // peers),
        out_shape=jax.ShapeDtypeStruct((kinds * tokens * pairs, width), fresh_qkv.dtype),
        in_specs=[ANY],
        out_specs=ANY,
        scratch_shapes=[
            pltpu.VMEM((PACK_STEPS, kinds, tokens, columns, width), fresh_qkv.dtype),
            pltpu.VMEM(part, F32),
            pltpu.VMEM(part, F32),
            pltpu.VMEM((PACK_STEPS, *part), fresh_qkv.dtype),
            pltpu.SemaphoreType.DMA((PACK_STEPS,)),
            pltpu.SemaphoreType.DMA((PACK_STEPS,)),
        ],
        compiler_params=pltpu.CompilerParams(vmem_limit_bytes=60 * MIB),
        cost_estimate=cost(6),
        name="pack",
    )(fresh_qkv)


def unpack_kernel(here, x_ref, q_out, fresh_out, wide, ordered, query, both, sems):
    length = query.shape[1]
    tokens = TOKENS
    peers = length // tokens
    wide[...] = x_ref[...].astype(F32)
    copies = []
    for kinds in ((1, 2), (0,)):
        for j in range(here):
            for c in kinds:
                for t in range(tokens):
                    row = (j * KINDS + c) * tokens + t
                    block = wide[pl.ds(row, peers, stride=here * KINDS * tokens), :]
                    ordered[c, pl.ds(t, peers, stride=tokens), :] = block
            if len(kinds) == 1:
                query[j] = ordered[0].astype(query.dtype)
                copy = pltpu.make_async_copy(query.at[j], q_out.at[j], sems.at[here + j])
            else:
                both[j] = ordered[1:].astype(both.dtype)
                copy = pltpu.make_async_copy(both.at[j], fresh_out.at[j], sems.at[j])
            copy.start()
            copies.append(copy)
    for copy in copies:
        copy.wait()


TOKENS = 18


def unpack(received, here):
    total, width = received.shape
    length = total // (KINDS * here)
    dtype = received.dtype
    shapes = [(here, length, width), (here, 2, length, width)]
    return pl.pallas_call(
        functools.partial(unpack_kernel, here),
        out_shape=[jax.ShapeDtypeStruct(shape, dtype) for shape in shapes],
        in_specs=[VMEM],
        out_specs=[ANY] * len(shapes),
        scratch_shapes=[
            pltpu.VMEM((total, width), F32),
            pltpu.VMEM((KINDS, length, width), F32),
            pltpu.VMEM((here, length, width), dtype),
            pltpu.VMEM((here, 2, length, width), dtype),
            pltpu.SemaphoreType.DMA((2 * here,)),
        ],
        compiler_params=pltpu.CompilerParams(vmem_limit_bytes=12 * MIB),
        cost_estimate=cost(5),
        name="unpack",
    )(received)


def attend_kernel(text_len, tokens, scalars, q_ref, fresh_ref, stale_ref, o_ref,
                  query, keys, values, scores, highest, result, sent, sems):
    here, length, width = q_ref.shape
    total = keys.shape[1]
    groups = total // length
    peers = length // tokens
    blocks = length // BLOCK
    scale = math.log2(math.e) / math.sqrt(width)
    own = scalars[0]
    text = pl.ds(pl.multiple_of(lax.rem(groups - own, groups) * length, length), text_len)
    lanes, ones = pl.ds(0, width), pl.ds(width, width)

    def fetch(pair):
        slot = pair % 2
        new = fresh_ref.at[pair]
        pairs = [(q_ref.at[pair], query.at[slot])]
        rows = pl.ds(0, length)
        pairs += [(new.at[0], keys.at[slot, rows, :]), (new.at[1], values.at[slot, rows, lanes])]
        for step in range(1, groups):
            group = lax.rem(own + step, groups)
            source = pl.ds(pl.multiple_of(group * length, length), length)
            rows = pl.ds(step * length, length)
            pairs += [
                (stale_ref.at[0, pair, source, :], keys.at[slot, rows, :]),
                (stale_ref.at[1, pair, source, :], values.at[slot, rows, lanes]),
            ]
        copies = [
            pltpu.make_async_copy(src, dst, sems.at[slot, i]) for i, (src, dst) in enumerate(pairs)
        ]
        for copy in copies:
            copy.start()
        return copies

    def attend_pair(pair):
        slot = pair % 2
        shown = lax.broadcasted_iota(jnp.int32, (text_len, width), 0) < scalars[1 + pair]
        text_keys = keys[slot, text, :].astype(F32)
        keys[slot, text, :] = jnp.where(shown, text_keys, text_keys[0:1]).astype(keys.dtype)
        text_values = values[slot, text, lanes].astype(F32)
        values[slot, text, lanes] = jnp.where(shown, text_values, 0.0).astype(values.dtype)
        values[slot, text, ones] = jnp.where(shown, 1.0, 0.0).astype(values.dtype)

        def score(i, side):
            rows = query[slot, pl.ds(i * BLOCK, BLOCK), :]
            dims = (((1,), (1,)), ((), ()))
            found = lax.dot_general(rows, keys[slot], dims, preferred_element_type=F32)
            scores[side] = found
            top = jnp.max(found, axis=1, keepdims=True)
            highest[side] = jnp.broadcast_to(top, (BLOCK, width))

        def weigh(i, side):
            top = highest[side][:, :1]
            weights = jnp.exp2((scores[side] - top) * scale).astype(values.dtype)
            summed = jnp.dot(weights, values[slot], preferred_element_type=F32)
            result[pl.ds(i * BLOCK, BLOCK), :] = summed[:, :width] / summed[:, width:]

        score(0, 0)
        for i in range(1, blocks):
            score(i, i % 2)
            weigh(i - 1, (i - 1) % 2)
        weigh(blocks - 1, (blocks - 1) % 2)
        for t in range(tokens):
            rows = pl.ds(pair * tokens + t, peers, stride=here * tokens)
            sent[rows, :] = result[pl.ds(t, peers, stride=tokens), :]

    waiting = fetch(0)
    values[:, :, ones] = jnp.ones((2, total, width), values.dtype)
    for pair in range(here):
        for copy in waiting:
            copy.wait()
        if pair + 1 < here:
            waiting = fetch(pair + 1)
        attend_pair(pair)
    o_ref[...] = sent[...].astype(o_ref.dtype)


PAIRS = 3


def attend(scalars, query, fresh, stale, text_len, tokens):
    here, length, width = query.shape
    total = stale.shape[2]
    groups = total // length
    return pl.pallas_call(
        functools.partial(attend_kernel, text_len, tokens),
        out_shape=jax.ShapeDtypeStruct((here * length, width), query.dtype),
        in_specs=[pl.BlockSpec(memory_space=pltpu.SMEM)] + [ANY] * 3,
        out_specs=VMEM,
        scratch_shapes=[
            pltpu.VMEM((2, length, width), query.dtype),
            pltpu.VMEM((2, total, width), query.dtype),
            pltpu.VMEM((2, total, 2 * width), query.dtype),
            pltpu.VMEM((2, BLOCK, total), F32),
            pltpu.VMEM((2, BLOCK, width), F32),
            pltpu.VMEM((length, width), F32),
            pltpu.VMEM((here * length, width), F32),
            pltpu.SemaphoreType.DMA((2, 1 + 2 * groups)),
        ],
        compiler_params=pltpu.CompilerParams(vmem_limit_bytes=56 * MIB),
        cost_estimate=cost(16, 8 * here * length * total * width, here * length * total),
        name="attend",
    )(scalars, query, fresh, stale)


def merge_kernel(x_ref, o_ref, wide, spread):
    tokens, pairs, _ = o_ref.shape
    here = PAIRS
    peers = pairs // here
    wide[...] = x_ref[...].astype(F32)
    for j in range(here):
        for t in range(tokens):
            block = wide[pl.ds(j * tokens + t, peers, stride=here * tokens), :]
            spread[pl.ds(t * pairs + j, peers, stride=here), :] = block
    o_ref[...] = spread[...].reshape(o_ref.shape).astype(o_ref.dtype)


def merge(moved, pairs):
    total, width = moved.shape
    return pl.pallas_call(
        merge_kernel,
        out_shape=jax.ShapeDtypeStruct((total // pairs, pairs, width), moved.dtype),
        in_specs=[VMEM],
        out_specs=VMEM,
        scratch_shapes=[pltpu.VMEM((total, width), F32)] * 2,
        compiler_params=pltpu.CompilerParams(vmem_limit_bytes=16 * MIB),
        cost_estimate=cost(2),
        name="merge",
    )(moved)


def place_kernel(scalars, own_ref, near_ref, far_ref, *refs):
    far_near_refs, (o_ref, rows, in_sems, out_sems) = refs[:-4], refs[-4:]
    kinds, here = o_ref.shape[:2]
    length = own_ref.shape[2]
    reads, writes = [], []
    for pair in range(here):
        for kind in range(kinds):
            copies = []
            parts = [ref.at[pair, kind] for ref in (own_ref, near_ref, far_ref)]
            for step, part in enumerate(parts + [far_near_refs[pair].at[kind]]):
                group = jnp.bitwise_xor(scalars[0], step)
                at = pl.ds(pl.multiple_of(group * length, length), length)
                copy = pltpu.make_async_copy(part, rows.at[kind, pair, at, :], in_sems.at[kind, pair, step])
                copy.start()
                copies.append(copy)
            reads.append((kind, pair, copies))
    for kind, pair, copies in reads:
        for copy in copies:
            copy.wait()
        copy = pltpu.make_async_copy(rows.at[kind, pair], o_ref.at[kind, pair], out_sems.at[kind, pair])
        copy.start()
        writes.append(copy)
    for copy in writes:
        copy.wait()


def place(scalars, parts, far_near, groups):
    here, kinds, length, width = parts[0].shape
    shape = (kinds, here, groups * length, width)
    return pl.pallas_call(
        place_kernel,
        out_shape=jax.ShapeDtypeStruct(shape, parts[0].dtype),
        in_specs=[pl.BlockSpec(memory_space=pltpu.SMEM)] + [ANY] * (len(parts) + here),
        out_specs=ANY,
        scratch_shapes=[
            pltpu.VMEM(shape, parts[0].dtype),
            pltpu.SemaphoreType.DMA((kinds, here, groups)),
            pltpu.SemaphoreType.DMA((kinds, here)),
        ],
        compiler_params=pltpu.CompilerParams(vmem_limit_bytes=16 * MIB),
        cost_estimate=cost(1),
        name="place",
    )(scalars, *parts, *far_near)


def exchange(rows):
    two_rows = rows.reshape(rows.shape[0] // 2, 2, rows.shape[1])
    moved = lax.all_to_all(two_rows, "seq", split_axis=0, concat_axis=0, tiled=True)
    return moved.reshape(rows.shape)


def swap(array, bit):
    groups = lax.axis_size("patch")
    return lax.ppermute(array, "patch", [(g, g ^ bit) for g in range(groups)])


def per_device(fresh_qkv, stale_kv, text_count):
    peers = lax.axis_size("seq")
    groups = lax.axis_size("patch")
    tokens, pairs = fresh_qkv.shape[1:3]
    here = pairs // peers
    seq_len = stale_kv.shape[1]
    text_len = TXT_DEV * seq_len // (TXT_DEV + IMG_DEV)
    first_pair = lax.axis_index("seq") * here
    image_index = (first_pair + jnp.arange(here)) // HEADS
    matches = image_index[:, None] == jnp.arange(text_count.shape[0])[None, :]
    valid_counts = jnp.sum(jnp.where(matches, text_count[None, :], 0), axis=1)
    own = lax.axis_index("patch").astype(jnp.int32)
    scalars = jnp.concatenate([own[None], valid_counts.astype(jnp.int32)])
    stale = jnp.transpose(stale_kv, (0, 2, 1, 3))

    sent, scalars = lax.optimization_barrier((pack(fresh_qkv, peers), scalars))
    query, fresh = unpack(exchange(sent), here)
    far = swap(fresh, 2)
    attended = attend(scalars, query, fresh, stale, text_len, tokens)
    moved = exchange(attended)
    far, _ = lax.optimization_barrier((far, attended))
    far_near = [swap(far[pair], 1) for pair in range(here)]
    refreshed = place(scalars, [fresh, swap(fresh, 1), far], far_near, groups)
    moved, refreshed = lax.optimization_barrier((moved, refreshed))
    result = merge(moved, pairs)
    return (result, jnp.transpose(refreshed, (0, 2, 1, 3)))


def solution(mesh):
    in_specs = (P(None, ("patch", "seq"), None, None), P(None, None, "seq", None), P())
    out_specs = (P(("patch", "seq"), None, None), P(None, None, "seq", None))
    return jax.shard_map(
        per_device, mesh=mesh, in_specs=in_specs, out_specs=out_specs, check_vma=False
    )
```

```python
import functools
import math

import jax
import jax.numpy as jnp
from jax import lax
from jax.experimental import pallas as pl
from jax.experimental.pallas import tpu as pltpu
from jax.sharding import PartitionSpec as P

HEADS = 24
TXT_DEV = 2
IMG_DEV = 16
KINDS = 3
PAIRS = 3
BLOCK = 576
MIB = 1024 * 1024
F32 = jnp.float32
VMEM = pl.BlockSpec(memory_space=pltpu.VMEM)
ANY = pl.BlockSpec(memory_space=pl.ANY)
HBM = pl.BlockSpec(memory_space=pltpu.HBM)


def cost(mib, flops=0, exps=0):
    return pl.CostEstimate(flops=flops, bytes_accessed=mib * MIB, transcendentals=exps)


def pack_kernel(here, chosen, x_ref, o_ref, read, wide, sent, packed, in_sems, out_sems):
    kinds, tokens, pairs, _ = x_ref.shape
    steps = in_sems.shape[0]
    columns = pairs // steps
    peers = columns // here
    rows = kinds * tokens * len(chosen)
    reads, writes = [], []
    for i in range(steps):
        part = pl.ds(i * columns, columns)
        copy = pltpu.make_async_copy(x_ref.at[:, :, part, :], read.at[i], in_sems.at[i])
        copy.start()
        reads.append(copy)
    for i in range(steps):
        reads[i].wait()
        wide[...] = read[i].astype(F32).reshape(wide.shape)
        for c in range(kinds):
            for t in range(tokens):
                for n, j in enumerate(chosen):
                    first = (c * tokens + t) * columns + j
                    row = (n * kinds + c) * tokens + t
                    sent[pl.ds(row, peers, stride=rows), :] = wide[pl.ds(first, peers, stride=here), :]
        packed[i] = sent[...].astype(packed.dtype)
        part = pl.ds(i * peers * rows, peers * rows)
        copy = pltpu.make_async_copy(packed.at[i], o_ref.at[part, :], out_sems.at[i])
        copy.start()
        writes.append(copy)
    for copy in writes:
        copy.wait()


PACK_STEPS = 4


def pack(fresh_qkv, peers, chosen):
    kinds, tokens, pairs, width = fresh_qkv.shape
    here = pairs // peers
    columns = pairs // PACK_STEPS
    rows = kinds * tokens * len(chosen)
    part = (rows * columns // here, width)
    return pl.pallas_call(
        functools.partial(pack_kernel, here, chosen),
        out_shape=jax.ShapeDtypeStruct((rows * peers, width), fresh_qkv.dtype),
        in_specs=[ANY],
        out_specs=ANY,
        scratch_shapes=[
            pltpu.VMEM((PACK_STEPS, kinds, tokens, columns, width), fresh_qkv.dtype),
            pltpu.VMEM((kinds * tokens * columns, width), F32),
            pltpu.VMEM(part, F32),
            pltpu.VMEM((PACK_STEPS, *part), fresh_qkv.dtype),
            pltpu.SemaphoreType.DMA((PACK_STEPS,)),
            pltpu.SemaphoreType.DMA((PACK_STEPS,)),
        ],
        compiler_params=pltpu.CompilerParams(vmem_limit_bytes=60 * MIB),
        cost_estimate=cost(6),
        name="pack",
    )(fresh_qkv)


def unpack_kernel(here, x_ref, q_ref, fresh_out, wide, ordered, both, sems):
    length = q_ref.shape[1]
    tokens = TOKENS
    peers = length // tokens
    wide[...] = x_ref[...].astype(F32)
    copies = []
    for kinds in ((1, 2), (0,)):
        for j in range(here):
            for c in kinds:
                for t in range(tokens):
                    row = (j * KINDS + c) * tokens + t
                    block = wide[pl.ds(row, peers, stride=here * KINDS * tokens), :]
                    ordered[c, pl.ds(t, peers, stride=tokens), :] = block
            if len(kinds) == 1:
                q_ref[j] = ordered[0].astype(q_ref.dtype)
            else:
                both[j] = ordered[1:].astype(both.dtype)
                copy = pltpu.make_async_copy(both.at[j], fresh_out.at[j], sems.at[j])
                copy.start()
                copies.append(copy)
    for copy in copies:
        copy.wait()


TOKENS = 18


def unpack(received, here):
    total, width = received.shape
    length = total // (KINDS * here)
    dtype = received.dtype
    shapes = [(here, length, width), (here, 2, length, width)]
    return pl.pallas_call(
        functools.partial(unpack_kernel, here),
        out_shape=[jax.ShapeDtypeStruct(shape, dtype) for shape in shapes],
        in_specs=[VMEM],
        out_specs=[VMEM, HBM],
        scratch_shapes=[
            pltpu.VMEM((total, width), F32),
            pltpu.VMEM((KINDS, length, width), F32),
            pltpu.VMEM((here, 2, length, width), dtype),
            pltpu.SemaphoreType.DMA((here,)),
        ],
        compiler_params=pltpu.CompilerParams(vmem_limit_bytes=16 * MIB),
        cost_estimate=cost(5),
        name="unpack",
    )(received)


def attend_kernel(text_len, tokens, first_pair, here, counts, q_ref, fresh_ref, stale_ref, done_ref, o_ref,
                  keys, values, scores, result, done, sent, sems, done_sem):
    count, length, width = q_ref.shape
    total = keys.shape[1]
    groups = total // length
    peers = length // tokens
    blocks = length // BLOCK
    scale = math.log2(math.e) / math.sqrt(width)
    last = first_pair + count == here
    own = lax.axis_index("patch").astype(jnp.int32)
    own_pair = lax.axis_index("seq").astype(jnp.int32) * here + first_pair
    text = pl.ds(pl.multiple_of(lax.rem(groups - own, groups) * length, length), text_len)
    lanes, ones = pl.ds(0, width), pl.ds(width, width)

    def fetch(pair):
        slot = pair % 2
        rows = pl.ds(0, length)
        pairs = [
            (fresh_ref.at[pair, 0], keys.at[slot, rows, :]),
            (fresh_ref.at[pair, 1], values.at[slot, rows, lanes]),
        ]
        for step in range(1, groups):
            group = lax.rem(own + step, groups)
            source = pl.ds(pl.multiple_of(group * length, length), length)
            rows = pl.ds(step * length, length)
            pairs += [
                (stale_ref.at[0, first_pair + pair, source, :], keys.at[slot, rows, :]),
                (stale_ref.at[1, first_pair + pair, source, :], values.at[slot, rows, lanes]),
            ]
        copies = [
            pltpu.make_async_copy(src, dst, sems.at[slot, i]) for i, (src, dst) in enumerate(pairs)
        ]
        for copy in copies:
            copy.start()
        return copies

    def lay_out(pair, source):
        for t in range(tokens):
            rows = pl.ds(pair * tokens + t, peers, stride=here * tokens)
            sent[rows, :] = source[pl.ds(t, peers, stride=tokens), :]

    def attend_pair(pair):
        slot = pair % 2
        valid = counts[(own_pair + pair) // HEADS]
        shown = lax.broadcasted_iota(jnp.int32, (text_len, width), 0) < valid
        text_keys = keys[slot, text, :].astype(F32)
        keys[slot, text, :] = jnp.where(shown, text_keys, text_keys[0:1]).astype(keys.dtype)
        text_values = values[slot, text, lanes].astype(F32)
        values[slot, text, lanes] = jnp.where(shown, text_values, 0.0).astype(values.dtype)
        values[slot, text, ones] = jnp.where(shown, 1.0, 0.0).astype(values.dtype)

        def score(i, side):
            rows = q_ref[pair, pl.ds(i * BLOCK, BLOCK), :]
            dims = (((1,), (1,)), ((), ()))
            top = None
            for at in range(0, total, CHUNK):
                part = keys[slot, pl.ds(at, CHUNK), :]
                found = lax.dot_general(rows, part, dims, preferred_element_type=F32)
                scores[side, :, pl.ds(at, CHUNK)] = found
                for lane in range(0, CHUNK, width):
                    piece = found[:, lane:lane + width]
                    top = piece if top is None else jnp.maximum(top, piece)
            return jnp.max(top, axis=1, keepdims=True)

        def weigh(i, side, top):
            summed = None
            for at in range(0, total, CHUNK):
                part = pl.ds(at, CHUNK)
                weights = jnp.exp2((scores[side, :, part] - top) * scale).astype(values.dtype)
                term = jnp.dot(weights, values[slot, part, :], preferred_element_type=F32)
                summed = term if summed is None else summed + term
            result[pl.ds(i * BLOCK, BLOCK), :] = summed[:, :width] / summed[:, width:]

        top = score(0, 0)
        for i in range(1, blocks):
            new_top = score(i, i % 2)
            weigh(i - 1, (i - 1) % 2, top)
            top = new_top
        weigh(blocks - 1, (blocks - 1) % 2, top)

    waiting = fetch(0)
    values[:, :, ones] = jnp.ones((2, total, width), values.dtype)
    if first_pair:
        earlier = pltpu.make_async_copy(done_ref, done, done_sem)
        earlier.start()
    for pair in range(count):
        for copy in waiting:
            copy.wait()
        if pair + 1 < count:
            waiting = fetch(pair + 1)
        attend_pair(pair)
        if last:
            lay_out(first_pair + pair, result)
        else:
            o_ref[pair] = result[...]
    if last:
        if first_pair:
            earlier.wait()
        for pair in range(first_pair):
            lay_out(pair, done.at[pair])
        o_ref[...] = sent[...].astype(o_ref.dtype)


CHUNK = 512


def attend(counts, query, fresh, stale, done, first_pair, text_len, tokens):
    count, length, width = query.shape
    here, total = stale.shape[1:3]
    groups = total // length
    last = first_pair + count == here
    if last:
        out_shape = jax.ShapeDtypeStruct((here * length, width), query.dtype)
    else:
        out_shape = jax.ShapeDtypeStruct(query.shape, F32)
    done = counts
    return pl.pallas_call(
        functools.partial(attend_kernel, text_len, tokens, first_pair, here),
        out_shape=out_shape,
        in_specs=[pl.BlockSpec(memory_space=pltpu.SMEM), VMEM, HBM, HBM, ANY],
        out_specs=VMEM,
        scratch_shapes=[
            pltpu.VMEM((2, total, width), query.dtype),
            pltpu.VMEM((2, total, 2 * width), query.dtype),
            pltpu.VMEM((2, BLOCK, total), F32),
            pltpu.VMEM((length, width), F32),
            pltpu.VMEM(done.shape, done.dtype),
            pltpu.VMEM((here * length, width), F32),
            pltpu.SemaphoreType.DMA((2, 2 * groups)),
            pltpu.SemaphoreType.DMA,
        ],
        compiler_params=pltpu.CompilerParams(vmem_limit_bytes=36 * MIB),
        cost_estimate=cost(16, 8 * count * length * total * width, count * length * total),
        name="attend",
    )(counts, query, fresh, stale, done)


def merge_kernel(x_ref, o_ref, wide, spread):
    tokens, pairs, _ = o_ref.shape
    here = PAIRS
    peers = pairs // here
    wide[...] = x_ref[...].astype(F32)
    for j in range(here):
        for t in range(tokens):
            block = wide[pl.ds(j * tokens + t, peers, stride=here * tokens), :]
            spread[pl.ds(t * pairs + j, peers, stride=here), :] = block
    o_ref[...] = spread[...].reshape(o_ref.shape).astype(o_ref.dtype)


def merge(moved, pairs):
    total, width = moved.shape
    return pl.pallas_call(
        merge_kernel,
        out_shape=jax.ShapeDtypeStruct((total // pairs, pairs, width), moved.dtype),
        in_specs=[VMEM],
        out_specs=VMEM,
        scratch_shapes=[pltpu.VMEM((total, width), F32)] * 2,
        compiler_params=pltpu.CompilerParams(vmem_limit_bytes=16 * MIB),
        cost_estimate=cost(2),
        name="merge",
    )(moved)


def place_kernel(groups, *refs):
    part_refs, (o_ref, rows, in_sems, out_sems) = refs[:-4], refs[-4:]
    kinds, here = o_ref.shape[:2]
    length = o_ref.shape[2] // groups
    own = lax.axis_index("patch").astype(jnp.int32)
    sources = [[ref.at[pair] for pair in range(here)] for ref in part_refs[: groups - 1]]
    sources.append([ref.at[0] for ref in part_refs[groups - 1 :]])
    reads, writes = [], []
    for pair in range(here):
        for kind in range(kinds):
            copies = []
            for step in range(groups):
                group = jnp.bitwise_xor(own, step)
                at = pl.ds(pl.multiple_of(group * length, length), length)
                copy = pltpu.make_async_copy(
                    sources[step][pair].at[kind], rows.at[kind, pair, at, :], in_sems.at[kind, pair, step]
                )
                copy.start()
                copies.append(copy)
            reads.append((kind, pair, copies))
    for kind, pair, copies in reads:
        for copy in copies:
            copy.wait()
        copy = pltpu.make_async_copy(rows.at[kind, pair], o_ref.at[kind, pair], out_sems.at[kind, pair])
        copy.start()
        writes.append(copy)
    for copy in writes:
        copy.wait()


def place(parts, far_near, here, groups):
    _, kinds, length, width = parts[0].shape
    shape = (kinds, here, groups * length, width)
    return pl.pallas_call(
        functools.partial(place_kernel, groups),
        out_shape=jax.ShapeDtypeStruct(shape, parts[0].dtype),
        in_specs=[ANY] * (len(parts) + here),
        out_specs=ANY,
        scratch_shapes=[
            pltpu.VMEM(shape, parts[0].dtype),
            pltpu.SemaphoreType.DMA((kinds, here, groups)),
            pltpu.SemaphoreType.DMA((kinds, here)),
        ],
        compiler_params=pltpu.CompilerParams(vmem_limit_bytes=16 * MIB),
        cost_estimate=cost(1),
        name="place",
    )(*parts, *far_near)


def exchange(rows):
    two_rows = rows.reshape(rows.shape[0] // 2, 2, rows.shape[1])
    moved = lax.all_to_all(two_rows, "seq", split_axis=0, concat_axis=0, tiled=True)
    return moved.reshape(rows.shape)


def swap(array, bit):
    groups = lax.axis_size("patch")
    return lax.ppermute(array, "patch", [(g, g ^ bit) for g in range(groups)])


def per_device(fresh_qkv, stale_kv, text_count):
    peers = lax.axis_size("seq")
    groups = lax.axis_size("patch")
    tokens, pairs = fresh_qkv.shape[1:3]
    here = pairs // peers
    seq_len = stale_kv.shape[1]
    text_len = TXT_DEV * seq_len // (TXT_DEV + IMG_DEV)
    stale = jnp.transpose(stale_kv, (0, 2, 1, 3))

    every = tuple(range(here))
    query, fresh = unpack(exchange(pack(fresh_qkv, peers, every)), here)
    far = swap(fresh, 2)
    attended = attend(text_count, query, fresh, stale, None, 0, text_len, tokens)
    moved = exchange(attended)
    far, _ = lax.optimization_barrier((far, attended))
    far_near = [swap(far[pair : pair + 1], 1) for pair in range(here)]
    refreshed = place([fresh, swap(fresh, 1), far], far_near, here, groups)
    moved, refreshed = lax.optimization_barrier((moved, refreshed))
    result = merge(moved, pairs)
    return (result, jnp.transpose(refreshed, (0, 2, 1, 3)))


def solution(mesh):
    in_specs = (P(None, ("patch", "seq"), None, None), P(None, None, "seq", None), P())
    out_specs = (P(("patch", "seq"), None, None), P(None, None, "seq", None))
    return jax.shard_map(
        per_device, mesh=mesh, in_specs=in_specs, out_specs=out_specs, check_vma=False
    )
```

```python
import functools
import math

import jax
import jax.numpy as jnp
from jax import lax
from jax.experimental import pallas as pl
from jax.experimental.pallas import tpu as pltpu
from jax.sharding import PartitionSpec as P

HEADS = 24
TXT_DEV = 2
IMG_DEV = 16
KINDS = 3
PAIRS = 3
BLOCK = 576
MIB = 1024 * 1024
F32 = jnp.float32
VMEM = pl.BlockSpec(memory_space=pltpu.VMEM)
ANY = pl.BlockSpec(memory_space=pl.ANY)
HBM = pl.BlockSpec(memory_space=pltpu.HBM)


def cost(mib, flops=0, exps=0):
    return pl.CostEstimate(flops=flops, bytes_accessed=mib * MIB, transcendentals=exps)


def pack_kernel(here, runs, x_ref, *refs):
    o_refs, (read, wide, sent, packed, in_sems, out_sems) = refs[: len(runs)], refs[len(runs) :]
    kinds, tokens, pairs, _ = x_ref.shape
    steps = in_sems.shape[0]
    columns = pairs // steps
    peers = columns // here
    reads, writes = [], []
    for i in range(steps):
        part = pl.ds(i * columns, columns)
        copy = pltpu.make_async_copy(x_ref.at[:, :, part, :], read.at[i], in_sems.at[i])
        copy.start()
        reads.append(copy)
    for i in range(steps):
        reads[i].wait()
        wide[...] = read[i].astype(F32).reshape(wide.shape)
        base = 0
        for k, run in enumerate(runs):
            rows = kinds * tokens * len(run)
            length = peers * rows
            for c in range(kinds):
                for t in range(tokens):
                    for n, j in enumerate(run):
                        first = (c * tokens + t) * columns + j
                        row = base + (n * kinds + c) * tokens + t
                        block = wide[pl.ds(first, peers, stride=here), :]
                        sent[pl.ds(row, peers, stride=rows), :] = block
            part = pl.ds(base, length)
            packed[i, part, :] = sent[part, :].astype(packed.dtype)
            copy = pltpu.make_async_copy(
                packed.at[i, part, :], o_refs[k].at[pl.ds(i * length, length), :], out_sems.at[i, k]
            )
            copy.start()
            writes.append(copy)
            base += length
    for copy in writes:
        copy.wait()


PACK_STEPS = 4


def pack(fresh_qkv, peers, runs):
    kinds, tokens, pairs, width = fresh_qkv.shape
    here = pairs // peers
    columns = pairs // PACK_STEPS
    part = (kinds * tokens * columns, width)
    shapes = [(kinds * tokens * len(run) * peers, width) for run in runs]
    return pl.pallas_call(
        functools.partial(pack_kernel, here, runs),
        out_shape=[jax.ShapeDtypeStruct(shape, fresh_qkv.dtype) for shape in shapes],
        in_specs=[ANY],
        out_specs=[ANY] * len(runs),
        scratch_shapes=[
            pltpu.VMEM((PACK_STEPS, kinds, tokens, columns, width), fresh_qkv.dtype),
            pltpu.VMEM(part, F32),
            pltpu.VMEM(part, F32),
            pltpu.VMEM((PACK_STEPS, *part), fresh_qkv.dtype),
            pltpu.SemaphoreType.DMA((PACK_STEPS,)),
            pltpu.SemaphoreType.DMA((PACK_STEPS, len(runs))),
        ],
        compiler_params=pltpu.CompilerParams(vmem_limit_bytes=60 * MIB),
        cost_estimate=cost(6),
        name="pack",
    )(fresh_qkv)


def unpack_kernel(here, x_ref, q_ref, fresh_out, wide, ordered, both, sems):
    length = q_ref.shape[1]
    tokens = TOKENS
    peers = length // tokens
    wide[...] = x_ref[...].astype(F32)
    copies = []
    for kinds in ((1, 2), (0,)):
        for j in range(here):
            for c in kinds:
                for t in range(tokens):
                    row = (j * KINDS + c) * tokens + t
                    block = wide[pl.ds(row, peers, stride=here * KINDS * tokens), :]
                    ordered[c, pl.ds(t, peers, stride=tokens), :] = block
            if len(kinds) == 1:
                q_ref[j] = ordered[0].astype(q_ref.dtype)
            else:
                both[j] = ordered[1:].astype(both.dtype)
                copy = pltpu.make_async_copy(both.at[j], fresh_out.at[j], sems.at[j])
                copy.start()
                copies.append(copy)
    for copy in copies:
        copy.wait()


TOKENS = 18


def unpack(received, here):
    total, width = received.shape
    length = total // (KINDS * here)
    dtype = received.dtype
    shapes = [(here, length, width), (here, 2, length, width)]
    return pl.pallas_call(
        functools.partial(unpack_kernel, here),
        out_shape=[jax.ShapeDtypeStruct(shape, dtype) for shape in shapes],
        in_specs=[VMEM],
        out_specs=[VMEM, HBM],
        scratch_shapes=[
            pltpu.VMEM((total, width), F32),
            pltpu.VMEM((KINDS, length, width), F32),
            pltpu.VMEM((here, 2, length, width), dtype),
            pltpu.SemaphoreType.DMA((here,)),
        ],
        compiler_params=pltpu.CompilerParams(vmem_limit_bytes=16 * MIB),
        cost_estimate=cost(5),
        name="unpack",
    )(received)


def attend_kernel(text_len, tokens, first_pair, here, counts, q_ref, fresh_ref, stale_ref, done_ref, o_ref,
                  keys, values, scores, result, done, sent, sems, done_sem):
    count, length, width = q_ref.shape
    total = keys.shape[1]
    groups = total // length
    peers = length // tokens
    blocks = length // BLOCK
    scale = math.log2(math.e) / math.sqrt(width)
    last = first_pair + count == here
    own = lax.axis_index("patch").astype(jnp.int32)
    own_pair = lax.axis_index("seq").astype(jnp.int32) * here + first_pair
    text = pl.ds(pl.multiple_of(lax.rem(groups - own, groups) * length, length), text_len)
    lanes, ones = pl.ds(0, width), pl.ds(width, width)

    def fetch(pair):
        slot = pair % 2
        chosen = first_pair + pair
        sides = []
        for kind, target in ((0, keys.at[slot]), (1, values.at[slot])):
            side = [(fresh_ref.at[pair, kind], target.at[pl.ds(0, length), lanes])]
            for step in range(1, groups):
                group = lax.rem(own + step, groups)
                source = pl.ds(pl.multiple_of(group * length, length), length)
                rows = pl.ds(step * length, length)
                side.append((stale_ref.at[kind, chosen, source, :], target.at[rows, lanes]))
            copies = [
                pltpu.make_async_copy(src, dst, sems.at[slot, kind * groups + i])
                for i, (src, dst) in enumerate(side)
            ]
            for copy in copies:
                copy.start()
            sides.append(copies)
        return sides

    def lay_out(pair, source):
        for t in range(tokens):
            rows = pl.ds(pair * tokens + t, peers, stride=here * tokens)
            sent[rows, :] = source[pl.ds(t, peers, stride=tokens), :]

    def attend_pair(pair, key_copies, value_copies):
        slot = pair % 2
        valid = counts[(own_pair + pair) // HEADS]
        shown = lax.broadcasted_iota(jnp.int32, (text_len, width), 0) < valid
        for copy in key_copies:
            copy.wait()
        text_keys = keys[slot, text, :].astype(F32)
        keys[slot, text, :] = jnp.where(shown, text_keys, text_keys[0:1]).astype(keys.dtype)
        values[slot, text, ones] = jnp.where(shown, 1.0, 0.0).astype(values.dtype)

        def score(i, side):
            rows = q_ref[pair, pl.ds(i * BLOCK, BLOCK), :]
            dims = (((1,), (1,)), ((), ()))
            top = None
            for at in range(0, total, CHUNK):
                part = keys[slot, pl.ds(at, CHUNK), :]
                found = lax.dot_general(rows, part, dims, preferred_element_type=F32)
                scores[side, :, pl.ds(at, CHUNK)] = found
                for lane in range(0, CHUNK, width):
                    piece = found[:, lane:lane + width]
                    top = piece if top is None else jnp.maximum(top, piece)
            return jnp.max(top, axis=1, keepdims=True)

        def weigh(i, side, top):
            summed = None
            for at in range(0, total, CHUNK):
                part = pl.ds(at, CHUNK)
                weights = jnp.exp2((scores[side, :, part] - top) * scale).astype(values.dtype)
                term = jnp.dot(weights, values[slot, part, :], preferred_element_type=F32)
                summed = term if summed is None else summed + term
            result[pl.ds(i * BLOCK, BLOCK), :] = summed[:, :width] / summed[:, width:]

        top = score(0, 0)
        for copy in value_copies:
            copy.wait()
        text_values = values[slot, text, lanes].astype(F32)
        values[slot, text, lanes] = jnp.where(shown, text_values, 0.0).astype(values.dtype)
        for i in range(1, blocks):
            new_top = score(i, i % 2)
            weigh(i - 1, (i - 1) % 2, top)
            top = new_top
        weigh(blocks - 1, (blocks - 1) % 2, top)

    waiting = fetch(0)
    values[:, :, ones] = jnp.ones((2, total, width), values.dtype)
    if first_pair:
        earlier = pltpu.make_async_copy(done_ref, done, done_sem)
        earlier.start()
    for pair in range(count):
        ready = waiting
        if pair + 1 < count:
            waiting = fetch(pair + 1)
        attend_pair(pair, *ready)
        if last:
            lay_out(first_pair + pair, result)
        else:
            o_ref[pair] = result[...]
    if last:
        if first_pair:
            earlier.wait()
        for pair in range(first_pair):
            lay_out(pair, done.at[pair])
        o_ref[...] = sent[...].astype(o_ref.dtype)


CHUNK = 512


def attend(counts, query, fresh, stale, done, first_pair, text_len, tokens):
    count, length, width = query.shape
    here, total = stale.shape[1:3]
    groups = total // length
    last = first_pair + count == here
    if last:
        out_shape = jax.ShapeDtypeStruct((here * length, width), query.dtype)
    else:
        out_shape = jax.ShapeDtypeStruct(query.shape, F32)
    if done is None:
        done = counts
    return pl.pallas_call(
        functools.partial(attend_kernel, text_len, tokens, first_pair, here),
        out_shape=out_shape,
        in_specs=[pl.BlockSpec(memory_space=pltpu.SMEM), VMEM, HBM, HBM, ANY],
        out_specs=VMEM,
        scratch_shapes=[
            pltpu.VMEM((2, total, width), query.dtype),
            pltpu.VMEM((2, total, 2 * width), query.dtype),
            pltpu.VMEM((2, BLOCK, total), F32),
            pltpu.VMEM((length, width), F32),
            pltpu.VMEM(done.shape, done.dtype),
            pltpu.VMEM((here * length, width), F32),
            pltpu.SemaphoreType.DMA((2, 2 * groups)),
            pltpu.SemaphoreType.DMA,
        ],
        compiler_params=pltpu.CompilerParams(vmem_limit_bytes=(57 if last else 36) * MIB),
        cost_estimate=cost(16, 8 * count * length * total * width, count * length * total),
        name="attend",
    )(counts, query, fresh, stale, done)


def merge_kernel(x_ref, o_ref, wide, spread):
    tokens, pairs, _ = o_ref.shape
    here = PAIRS
    peers = pairs // here
    wide[...] = x_ref[...].astype(F32)
    for j in range(here):
        for t in range(tokens):
            block = wide[pl.ds(j * tokens + t, peers, stride=here * tokens), :]
            spread[pl.ds(t * pairs + j, peers, stride=here), :] = block
    o_ref[...] = spread[...].reshape(o_ref.shape).astype(o_ref.dtype)


def merge(moved, pairs):
    total, width = moved.shape
    return pl.pallas_call(
        merge_kernel,
        out_shape=jax.ShapeDtypeStruct((total // pairs, pairs, width), moved.dtype),
        in_specs=[VMEM],
        out_specs=VMEM,
        scratch_shapes=[pltpu.VMEM((total, width), F32)] * 2,
        compiler_params=pltpu.CompilerParams(vmem_limit_bytes=16 * MIB),
        cost_estimate=cost(2),
        name="merge",
    )(moved)


def place_kernel(groups, *refs):
    part_refs, (o_ref, rows, in_sems, out_sems) = refs[:-4], refs[-4:]
    kinds, here = o_ref.shape[:2]
    length = o_ref.shape[2] // groups
    own = lax.axis_index("patch").astype(jnp.int32)
    sources = [[] for _ in range(groups)]
    for i, ref in enumerate(part_refs):
        sources[i % groups] += [ref.at[pair] for pair in range(ref.shape[0])]
    reads, writes = [], []
    for pair in range(here):
        for kind in range(kinds):
            copies = []
            for step in range(groups):
                group = jnp.bitwise_xor(own, step)
                at = pl.ds(pl.multiple_of(group * length, length), length)
                copy = pltpu.make_async_copy(
                    sources[step][pair].at[kind], rows.at[kind, pair, at, :], in_sems.at[kind, pair, step]
                )
                copy.start()
                copies.append(copy)
            reads.append((kind, pair, copies))
    for kind, pair, copies in reads:
        for copy in copies:
            copy.wait()
        copy = pltpu.make_async_copy(rows.at[kind, pair], o_ref.at[kind, pair], out_sems.at[kind, pair])
        copy.start()
        writes.append(copy)
    for copy in writes:
        copy.wait()


def place(parts, here, groups):
    _, kinds, length, width = parts[0].shape
    shape = (kinds, here, groups * length, width)
    return pl.pallas_call(
        functools.partial(place_kernel, groups),
        out_shape=jax.ShapeDtypeStruct(shape, parts[0].dtype),
        in_specs=[ANY] * len(parts),
        out_specs=ANY,
        scratch_shapes=[
            pltpu.VMEM(shape, parts[0].dtype),
            pltpu.SemaphoreType.DMA((kinds, here, groups)),
            pltpu.SemaphoreType.DMA((kinds, here)),
        ],
        compiler_params=pltpu.CompilerParams(vmem_limit_bytes=16 * MIB),
        cost_estimate=cost(1),
        name="place",
    )(*parts)


def exchange(rows):
    two_rows = rows.reshape(rows.shape[0] // 2, 2, rows.shape[1])
    moved = lax.all_to_all(two_rows, "seq", split_axis=0, concat_axis=0, tiled=True)
    return moved.reshape(rows.shape)


def swap(array, bit):
    groups = lax.axis_size("patch")
    return lax.ppermute(array, "patch", [(g, g ^ bit) for g in range(groups)])


def per_device(fresh_qkv, stale_kv, text_count):
    peers = lax.axis_size("seq")
    groups = lax.axis_size("patch")
    tokens, pairs = fresh_qkv.shape[1:3]
    here = pairs // peers
    seq_len = stale_kv.shape[1]
    text_len = TXT_DEV * seq_len // (TXT_DEV + IMG_DEV)
    stale = jnp.transpose(stale_kv, (0, 2, 1, 3))

    early, late = tuple(range(here - 1)), (here - 1,)
    early_sent, late_sent = pack(fresh_qkv, peers, (early, late))
    query, fresh = unpack(exchange(early_sent), len(early))
    late_sent, query = lax.optimization_barrier((late_sent, query))
    received = exchange(late_sent)
    far = swap(fresh, 2)
    done = attend(text_count, query, fresh, stale, None, 0, text_len, tokens)
    received, done = lax.optimization_barrier((received, done))
    query, late_fresh = unpack(received, len(late))
    late_far = swap(late_fresh, 2)
    attended = attend(text_count, query, late_fresh, stale, done, len(early), text_len, tokens)
    moved = exchange(attended)
    far, late_far, _ = lax.optimization_barrier((far, late_far, attended))
    parts = [fresh, swap(fresh, 1), far, swap(far, 1)]
    parts += [late_fresh, swap(late_fresh, 1), late_far, swap(late_far, 1)]
    refreshed = place(parts, here, groups)
    moved, refreshed = lax.optimization_barrier((moved, refreshed))
    result = merge(moved, pairs)
    return (result, jnp.transpose(refreshed, (0, 2, 1, 3)))


def solution(mesh):
    in_specs = (P(None, ("patch", "seq"), None, None), P(None, None, "seq", None), P())
    out_specs = (P(("patch", "seq"), None, None), P(None, None, "seq", None))
    return jax.shard_map(
        per_device, mesh=mesh, in_specs=in_specs, out_specs=out_specs, check_vma=False
    )
```

```python
import functools
import math

import jax
import jax.numpy as jnp
from jax import lax
from jax.experimental import pallas as pl
from jax.experimental.pallas import tpu as pltpu
from jax.sharding import PartitionSpec as P

HEADS = 24
TXT_DEV = 2
IMG_DEV = 16
KINDS = 3
PAIRS = 3
BLOCK = 576
MIB = 1024 * 1024
F32 = jnp.float32
VMEM = pl.BlockSpec(memory_space=pltpu.VMEM)
ANY = pl.BlockSpec(memory_space=pl.ANY)
HBM = pl.BlockSpec(memory_space=pltpu.HBM)


def cost(mib, flops=0, exps=0):
    return pl.CostEstimate(flops=flops, bytes_accessed=mib * MIB, transcendentals=exps)


def pack_kernel(here, runs, x_ref, *refs):
    o_refs, (read, wide, sent, packed, in_sems, out_sems) = refs[: len(runs)], refs[len(runs) :]
    kinds, tokens, pairs, _ = x_ref.shape
    steps = in_sems.shape[0]
    columns = pairs // steps
    peers = columns // here
    reads, writes = [], []
    for i in range(steps):
        part = pl.ds(i * columns, columns)
        copy = pltpu.make_async_copy(x_ref.at[:, :, part, :], read.at[i], in_sems.at[i])
        copy.start()
        reads.append(copy)
    for i in range(steps):
        reads[i].wait()
        wide[...] = read[i].astype(F32).reshape(wide.shape)
        base = 0
        for k, run in enumerate(runs):
            rows = kinds * tokens * len(run)
            length = peers * rows
            for c in range(kinds):
                for t in range(tokens):
                    for n, j in enumerate(run):
                        first = (c * tokens + t) * columns + j
                        row = base + (n * kinds + c) * tokens + t
                        block = wide[pl.ds(first, peers, stride=here), :]
                        sent[pl.ds(row, peers, stride=rows), :] = block
            part = pl.ds(base, length)
            packed[i, part, :] = sent[part, :].astype(packed.dtype)
            copy = pltpu.make_async_copy(
                packed.at[i, part, :], o_refs[k].at[pl.ds(i * length, length), :], out_sems.at[i, k]
            )
            copy.start()
            writes.append(copy)
            base += length
    for copy in writes:
        copy.wait()


PACK_STEPS = 4


def pack(fresh_qkv, peers, runs):
    kinds, tokens, pairs, width = fresh_qkv.shape
    here = pairs // peers
    columns = pairs // PACK_STEPS
    part = (kinds * tokens * columns, width)
    shapes = [(kinds * tokens * len(run) * peers, width) for run in runs]
    return pl.pallas_call(
        functools.partial(pack_kernel, here, runs),
        out_shape=[jax.ShapeDtypeStruct(shape, fresh_qkv.dtype) for shape in shapes],
        in_specs=[ANY],
        out_specs=[ANY] * len(runs),
        scratch_shapes=[
            pltpu.VMEM((PACK_STEPS, kinds, tokens, columns, width), fresh_qkv.dtype),
            pltpu.VMEM(part, F32),
            pltpu.VMEM(part, F32),
            pltpu.VMEM((PACK_STEPS, *part), fresh_qkv.dtype),
            pltpu.SemaphoreType.DMA((PACK_STEPS,)),
            pltpu.SemaphoreType.DMA((PACK_STEPS, len(runs))),
        ],
        compiler_params=pltpu.CompilerParams(vmem_limit_bytes=60 * MIB),
        cost_estimate=cost(6),
        name="pack",
    )(fresh_qkv)


def unpack_kernel(here, x_ref, q_out, fresh_out, wide, ordered, query, both, sems):
    length = query.shape[1]
    tokens = TOKENS
    peers = length // tokens
    wide[...] = x_ref[...].astype(F32)
    copies = []
    for kinds in ((1, 2), (0,)):
        for j in range(here):
            for c in kinds:
                for t in range(tokens):
                    row = (j * KINDS + c) * tokens + t
                    block = wide[pl.ds(row, peers, stride=here * KINDS * tokens), :]
                    ordered[c, pl.ds(t, peers, stride=tokens), :] = block
            if len(kinds) == 1:
                query[j] = ordered[0].astype(query.dtype)
                copy = pltpu.make_async_copy(query.at[j], q_out.at[j], sems.at[here + j])
            else:
                both[j] = ordered[1:].astype(both.dtype)
                copy = pltpu.make_async_copy(both.at[j], fresh_out.at[j], sems.at[j])
            copy.start()
            copies.append(copy)
    for copy in copies:
        copy.wait()


TOKENS = 18


def unpack(received, here):
    total, width = received.shape
    length = total // (KINDS * here)
    dtype = received.dtype
    shapes = [(here, length, width), (here, 2, length, width)]
    return pl.pallas_call(
        functools.partial(unpack_kernel, here),
        out_shape=[jax.ShapeDtypeStruct(shape, dtype) for shape in shapes],
        in_specs=[VMEM],
        out_specs=[HBM, HBM],
        scratch_shapes=[
            pltpu.VMEM((total, width), F32),
            pltpu.VMEM((KINDS, length, width), F32),
            pltpu.VMEM((here, length, width), dtype),
            pltpu.VMEM((here, 2, length, width), dtype),
            pltpu.SemaphoreType.DMA((2 * here,)),
        ],
        compiler_params=pltpu.CompilerParams(vmem_limit_bytes=16 * MIB),
        cost_estimate=cost(5),
        name="unpack",
    )(received)


def attend_kernel(text_len, tokens, first_pair, here, counts, q_ref, fresh_ref, stale_ref, done_ref, o_ref,
                  query, keys, values, scores, result, done, sent, sems, done_sem):
    count, length, width = q_ref.shape
    total = keys.shape[1]
    groups = total // length
    peers = length // tokens
    blocks = length // BLOCK
    scale = math.log2(math.e) / math.sqrt(width)
    last = first_pair + count == here
    own = lax.axis_index("patch").astype(jnp.int32)
    own_pair = lax.axis_index("seq").astype(jnp.int32) * here + first_pair
    text = pl.ds(pl.multiple_of(lax.rem(groups - own, groups) * length, length), text_len)
    lanes, ones = pl.ds(0, width), pl.ds(width, width)

    def fetch(pair):
        slot = pair % 2
        chosen = first_pair + pair
        sides = []
        for kind, target in ((0, keys.at[slot]), (1, values.at[slot])):
            side = [(fresh_ref.at[pair, kind], target.at[pl.ds(0, length), lanes])]
            if kind == 0:
                side.append((q_ref.at[pair], query.at[slot]))
            for step in range(1, groups):
                group = lax.rem(own + step, groups)
                source = pl.ds(pl.multiple_of(group * length, length), length)
                rows = pl.ds(step * length, length)
                side.append((stale_ref.at[kind, chosen, source, :], target.at[rows, lanes]))
            copies = [
                pltpu.make_async_copy(src, dst, sems.at[slot, kind * (groups + 1) + i])
                for i, (src, dst) in enumerate(side)
            ]
            for copy in copies:
                copy.start()
            sides.append(copies)
        return sides

    def lay_out(pair, source):
        for t in range(tokens):
            rows = pl.ds(pair * tokens + t, peers, stride=here * tokens)
            sent[rows, :] = source[pl.ds(t, peers, stride=tokens), :]

    def attend_pair(pair, key_copies, value_copies):
        slot = pair % 2
        valid = counts[(own_pair + pair) // HEADS]
        shown = lax.broadcasted_iota(jnp.int32, (text_len, width), 0) < valid
        for copy in key_copies:
            copy.wait()
        text_keys = keys[slot, text, :].astype(F32)
        keys[slot, text, :] = jnp.where(shown, text_keys, text_keys[0:1]).astype(keys.dtype)
        values[slot, text, ones] = jnp.where(shown, 1.0, 0.0).astype(values.dtype)

        def score(i, side):
            rows = query[slot, pl.ds(i * BLOCK, BLOCK), :]
            dims = (((1,), (1,)), ((), ()))
            top = None
            for at in range(0, total, CHUNK):
                part = keys[slot, pl.ds(at, CHUNK), :]
                found = lax.dot_general(rows, part, dims, preferred_element_type=F32)
                scores[side, :, pl.ds(at, CHUNK)] = found
                for lane in range(0, CHUNK, width):
                    piece = found[:, lane:lane + width]
                    top = piece if top is None else jnp.maximum(top, piece)
            return jnp.max(top, axis=1, keepdims=True)

        def weigh(i, side, top):
            summed = None
            for at in range(0, total, CHUNK):
                part = pl.ds(at, CHUNK)
                weights = jnp.exp2((scores[side, :, part] - top) * scale).astype(values.dtype)
                term = jnp.dot(weights, values[slot, part, :], preferred_element_type=F32)
                summed = term if summed is None else summed + term
            result[pl.ds(i * BLOCK, BLOCK), :] = summed[:, :width] / summed[:, width:]

        top = score(0, 0)
        for copy in value_copies:
            copy.wait()
        text_values = values[slot, text, lanes].astype(F32)
        values[slot, text, lanes] = jnp.where(shown, text_values, 0.0).astype(values.dtype)
        if last and pair == 0:
            lay_out_earlier()
        for i in range(1, blocks):
            new_top = score(i, i % 2)
            weigh(i - 1, (i - 1) % 2, top)
            top = new_top
        weigh(blocks - 1, (blocks - 1) % 2, top)

    def lay_out_earlier():
        if first_pair:
            earlier.wait()
        for pair in range(first_pair):
            lay_out(pair, done.at[pair])

    waiting = fetch(0)
    values[:, :, ones] = jnp.ones((2, total, width), values.dtype)
    if first_pair:
        earlier = pltpu.make_async_copy(done_ref, done, done_sem)
        earlier.start()
    for pair in range(count):
        ready = waiting
        if pair + 1 < count:
            waiting = fetch(pair + 1)
        attend_pair(pair, *ready)
        if last:
            lay_out(first_pair + pair, result)
        else:
            o_ref[pair] = result[...]
    if last:
        o_ref[...] = sent[...].astype(o_ref.dtype)


CHUNK = 512


def attend(counts, query, fresh, stale, done, first_pair, text_len, tokens):
    count, length, width = query.shape
    here, total = stale.shape[1:3]
    groups = total // length
    last = first_pair + count == here
    if last:
        out_shape = jax.ShapeDtypeStruct((here * length, width), query.dtype)
    else:
        out_shape = jax.ShapeDtypeStruct(query.shape, F32)
    if done is None:
        done = counts
    return pl.pallas_call(
        functools.partial(attend_kernel, text_len, tokens, first_pair, here),
        out_shape=out_shape,
        in_specs=[pl.BlockSpec(memory_space=pltpu.SMEM), HBM, HBM, HBM, ANY],
        out_specs=VMEM,
        scratch_shapes=[
            pltpu.VMEM((2, length, width), query.dtype),
            pltpu.VMEM((2, total, width), query.dtype),
            pltpu.VMEM((2, total, 2 * width), query.dtype),
            pltpu.VMEM((2, BLOCK, total), F32),
            pltpu.VMEM((length, width), F32),
            pltpu.VMEM(done.shape, done.dtype),
            pltpu.VMEM((here * length, width), F32),
            pltpu.SemaphoreType.DMA((2, 2 * groups + 1)),
            pltpu.SemaphoreType.DMA,
        ],
        compiler_params=pltpu.CompilerParams(vmem_limit_bytes=(57 if last else 36) * MIB),
        cost_estimate=cost(16, 8 * count * length * total * width, count * length * total),
        name="attend",
    )(counts, query, fresh, stale, done)


def merge_kernel(x_ref, o_ref, wide, spread):
    tokens, pairs, _ = o_ref.shape
    here = PAIRS
    peers = pairs // here
    wide[...] = x_ref[...].astype(F32)
    for j in range(here):
        for t in range(tokens):
            block = wide[pl.ds(j * tokens + t, peers, stride=here * tokens), :]
            spread[pl.ds(t * pairs + j, peers, stride=here), :] = block
    o_ref[...] = spread[...].reshape(o_ref.shape).astype(o_ref.dtype)


def merge(moved, pairs):
    total, width = moved.shape
    return pl.pallas_call(
        merge_kernel,
        out_shape=jax.ShapeDtypeStruct((total // pairs, pairs, width), moved.dtype),
        in_specs=[VMEM],
        out_specs=VMEM,
        scratch_shapes=[pltpu.VMEM((total, width), F32)] * 2,
        compiler_params=pltpu.CompilerParams(vmem_limit_bytes=16 * MIB),
        cost_estimate=cost(2),
        name="merge",
    )(moved)


def place_kernel(groups, *refs):
    part_refs, (o_ref, rows, in_sems, out_sems) = refs[:-4], refs[-4:]
    kinds, here = o_ref.shape[:2]
    length = o_ref.shape[2] // groups
    own = lax.axis_index("patch").astype(jnp.int32)
    sources = [[] for _ in range(groups)]
    for i, ref in enumerate(part_refs):
        sources[i % groups] += [ref.at[pair] for pair in range(ref.shape[0])]
    reads, writes = [], []
    for pair in range(here):
        for kind in range(kinds):
            copies = []
            for step in range(groups):
                group = jnp.bitwise_xor(own, step)
                at = pl.ds(pl.multiple_of(group * length, length), length)
                copy = pltpu.make_async_copy(
                    sources[step][pair].at[kind], rows.at[kind, pair, at, :], in_sems.at[kind, pair, step]
                )
                copy.start()
                copies.append(copy)
            reads.append((kind, pair, copies))
    for kind, pair, copies in reads:
        for copy in copies:
            copy.wait()
        copy = pltpu.make_async_copy(rows.at[kind, pair], o_ref.at[kind, pair], out_sems.at[kind, pair])
        copy.start()
        writes.append(copy)
    for copy in writes:
        copy.wait()


def place(parts, here, groups):
    _, kinds, length, width = parts[0].shape
    shape = (kinds, here, groups * length, width)
    return pl.pallas_call(
        functools.partial(place_kernel, groups),
        out_shape=jax.ShapeDtypeStruct(shape, parts[0].dtype),
        in_specs=[ANY] * len(parts),
        out_specs=ANY,
        scratch_shapes=[
            pltpu.VMEM(shape, parts[0].dtype),
            pltpu.SemaphoreType.DMA((kinds, here, groups)),
            pltpu.SemaphoreType.DMA((kinds, here)),
        ],
        compiler_params=pltpu.CompilerParams(vmem_limit_bytes=16 * MIB),
        cost_estimate=cost(1),
        name="place",
    )(*parts)


def exchange(rows):
    two_rows = rows.reshape(rows.shape[0] // 2, 2, rows.shape[1])
    moved = lax.all_to_all(two_rows, "seq", split_axis=0, concat_axis=0, tiled=True)
    return moved.reshape(rows.shape)


def swap(array, bit):
    groups = lax.axis_size("patch")
    return lax.ppermute(array, "patch", [(g, g ^ bit) for g in range(groups)])


def per_device(fresh_qkv, stale_kv, text_count):
    peers = lax.axis_size("seq")
    groups = lax.axis_size("patch")
    tokens, pairs = fresh_qkv.shape[1:3]
    here = pairs // peers
    seq_len = stale_kv.shape[1]
    text_len = TXT_DEV * seq_len // (TXT_DEV + IMG_DEV)
    stale = jnp.transpose(stale_kv, (0, 2, 1, 3))

    early, late = tuple(range(here - 1)), (here - 1,)
    early_sent, late_sent = pack(fresh_qkv, peers, (early, late))
    query, fresh = unpack(exchange(early_sent), len(early))
    late_sent, query = lax.optimization_barrier((late_sent, query))
    received = exchange(late_sent)
    far = swap(fresh, 2)
    done = attend(text_count, query, fresh, stale, None, 0, text_len, tokens)
    received, done = lax.optimization_barrier((received, done))
    query, late_fresh = unpack(received, len(late))
    late_far = swap(late_fresh, 2)
    attended = attend(text_count, query, late_fresh, stale, done, len(early), text_len, tokens)
    moved = exchange(attended)
    far, late_far, _ = lax.optimization_barrier((far, late_far, attended))
    parts = [fresh, swap(fresh, 1), far, swap(far, 1)]
    parts += [late_fresh, swap(late_fresh, 1), late_far, swap(late_far, 1)]
    refreshed = place(parts, here, groups)
    moved, refreshed = lax.optimization_barrier((moved, refreshed))
    result = merge(moved, pairs)
    return (result, jnp.transpose(refreshed, (0, 2, 1, 3)))


def solution(mesh):
    in_specs = (P(None, ("patch", "seq"), None, None), P(None, None, "seq", None), P())
    out_specs = (P(("patch", "seq"), None, None), P(None, None, "seq", None))
    return jax.shard_map(
        per_device, mesh=mesh, in_specs=in_specs, out_specs=out_specs, check_vma=False
    )
```
